32 devices in a mesh: grp: 2 (over x), wide: 16 (over z, y, core).
Axes of the slice: x: 2, y: 2, z: 4, core: 2. Of those that a mesh axis runs over, the one named last changes fastest.
Arguments:
- xblocks: bfloat16 [128, 64, 64], P(('grp', 'wide')), parts along dimension 0, may hold values from -6 to 6
- pattern: int32 [3, 128], P(None, ('grp', 'wide')), parts along dimension 1, may hold values from 0 to 31, as said below
- counts: int32 [32], P(('grp', 'wide')), parts along dimension 0, may hold values from 1 to 4, as said below
- coef: bfloat16 [2048, 4096], P(None, 'wide'), may hold values from -0.25 to 0.25
Outputs:
- features: bfloat16 [16, 4096, 4096], P('grp', 'wide'), parts along dimension 0
The draws below stay inside these ranges and needn't reach their ends.
There are 2 independent parts, one for each index of `grp`. The reference program is written for one: setup_inputs(seed, part) draws one part's arguments, and reference() takes and returns one part's arrays. A program takes and returns all parts, laid end to end along the dimension named above; an argument that names none is the same for every part. Nothing has to cross between parts.
Inputs may be any that keep to these rules, and one draw needn't show every extreme that they name: pattern[0] is the pair (below 8), pattern[1] and pattern[2] the bra and ket AO blocks (below 32); no triple occurs twice. `counts`: slots at and after a device's count are not part of the problem.
All inputs are finite; a program needn't handle non-finite values.
Results may differ from the reference program's by a relative error of at most 0.0051.
Values may be sent and summed in bfloat16 or wider, within the bound.
A program may use at most 128 MiB of HBM per device.

```python
import jax
import jax.numpy as jnp
from jax import lax

BLOCK_ORBITALS = 64
DOMAIN_BLOCKS = 32
VIRTUAL_COUNT = 4096
PAIR_COUNT = 8
DEVICE_SLOTS = 4
NAO = 2048
SLOTS = 64
N_WIDE = 16


def draw_pattern(key, part):
    key = jax.random.fold_in(key, 7)
    selected_blocks = jax.random.permutation(key, PAIR_COUNT * DOMAIN_BLOCKS * DOMAIN_BLOCKS)[:N_WIDE * DEVICE_SLOTS].astype(jnp.int32)
    pair_row = selected_blocks // (DOMAIN_BLOCKS * DOMAIN_BLOCKS)
    bra_row = selected_blocks // DOMAIN_BLOCKS % DOMAIN_BLOCKS
    ket_row = selected_blocks % DOMAIN_BLOCKS
    return jnp.stack([pair_row, bra_row, ket_row]).astype(jnp.int32)


def draw_counts(key, part):
    key = jax.random.fold_in(key, 11)
    random_key_seed, key_full, key_force = jax.random.split(key, 3)
    offset_start = jax.random.randint(random_key_seed, (N_WIDE,), 1, DEVICE_SLOTS // 2 + 1)
    occupied_slots = jax.random.randint(key_full, (N_WIDE,), 0, 6) == 0
    forced = jax.random.randint(key_force, (), 0, N_WIDE)
    occupied_slots = occupied_slots | (jnp.arange(N_WIDE) == forced)
    return jnp.where(occupied_slots, DEVICE_SLOTS, offset_start).astype(jnp.int32)


def steps_of(own_key, shape, pieces, smallest, top_value):
    def one(position, shards_of):
        draws = jax.random.uniform(jax.random.fold_in(jax.random.fold_in(own_key, 6), position), (shards_of,), jnp.float32, smallest / len(pieces), top_value / len(pieces))
        return jnp.repeat(jnp.exp(draws), shape[position] // shards_of).reshape((-1,) + (1,) * (len(shape) - position - 1))

    loudness = one(*pieces[0])
    for cut in pieces[1:]:
        loudness = loudness * one(*cut)
    return loudness


def noise(key, shape, deviation, bound, pieces=(), kind=jnp.bfloat16):
    array = jax.random.normal(key, shape, jnp.float32) * deviation
    if len(pieces) > 0:
        array = steps_of(key, shape, pieces, -0.22, 0.18) * array
    return jnp.clip(array, min=-bound, max=bound).astype(kind)


def setup_inputs(seed: int = 0, part: int = 0) -> dict:
    key_list = jax.random.split(jax.random.key(seed), 5)
    part_splits = jax.random.split(jax.random.fold_in(key_list[4], part), 5)
    return {
        "xblocks": noise(part_splits[0], (SLOTS, BLOCK_ORBITALS, BLOCK_ORBITALS), 1.0, 6.0, ((0, 16),)),
        "pattern": draw_pattern(jax.random.fold_in(jax.random.fold_in(key_list[4], part), 71), part),
        "counts": draw_counts(jax.random.fold_in(jax.random.fold_in(key_list[4], part), 71), part),
        "coef": noise(key_list[3], (NAO, VIRTUAL_COUNT), (8 * BLOCK_ORBITALS) ** -0.5, 0.25, ((1, 16),)),
    }


def reference(xblocks, pattern, counts, coef):
    slot_index = jnp.arange(N_WIDE * DEVICE_SLOTS, dtype=jnp.int32)
    active_mask = (slot_index % DEVICE_SLOTS) < jnp.repeat(counts, DEVICE_SLOTS)
    destination = jnp.where(active_mask, pattern[0] * DOMAIN_BLOCKS + pattern[1], PAIR_COUNT * DOMAIN_BLOCKS).astype(jnp.int32)
    rows = coef.reshape(DOMAIN_BLOCKS, BLOCK_ORBITALS, VIRTUAL_COUNT)
    group_exchange = xblocks.reshape(N_WIDE, DEVICE_SLOTS, BLOCK_ORBITALS, BLOCK_ORBITALS)
    group_sender = pattern[2].reshape(N_WIDE, DEVICE_SLOTS)
    group_target = destination.reshape(N_WIDE, DEVICE_SLOTS)

    def step(acc, item):
        blocks, sigma, tgt = item
        picked = rows[sigma]
        contribution = jnp.einsum("sij,sjv->siv", blocks.astype(jnp.float32), picked.astype(jnp.float32)).astype(jnp.bfloat16)
        acc = acc.at[tgt].add(contribution.astype(jnp.float32))
        return acc, None

    start = jnp.zeros((PAIR_COUNT * DOMAIN_BLOCKS + 1, BLOCK_ORBITALS, VIRTUAL_COUNT), jnp.float32)
    acc, unused = lax.scan(step, start, (group_exchange, group_sender, group_target))
    half = acc[: PAIR_COUNT * DOMAIN_BLOCKS].astype(jnp.bfloat16).reshape(PAIR_COUNT, NAO, VIRTUAL_COUNT)

    def final(half_pair):
        return jnp.dot(half_pair.T, coef, preferred_element_type=jnp.float32).astype(jnp.bfloat16)

    return lax.map(final, half)
```

```python
import functools

import jax
import jax.numpy as jnp
from jax import lax
from jax.experimental import pallas as pl
from jax.experimental.pallas import tpu as pltpu
from jax.sharding import PartitionSpec as P

DOMAIN_BLOCKS = 32
PAIR_COUNT = 8
MESH = pl.DeviceIdType.MESH
PAYLOAD = 4
CHUNKS = 5
UP, DOWN, Y, X, CORE = range(5)


def gather_kernel(nz, coef_ref, pay_ref, full_ref, pays_ref, send_sem, recv_sem, local_sem):
    x = lax.axis_index("grp")
    wide = lax.axis_index("wide")
    z, y, core = lax.div(wide, 4), lax.rem(lax.div(wide, 2), 2), lax.rem(wide, 2)
    other = 1 - y
    quarter = coef_ref.shape[0] // 4

    def index(zz, yy, cc):
        return (zz * 2 + yy) * 2 + cc

    device = {
        UP: {"wide": wide + 4},
        DOWN: {"wide": wide - 4},
        Y: {"wide": index(z, 1 - y, core)},
        X: {"grp": 1 - x},
        CORE: {"wide": index(z, y, 1 - core)},
    }
    barrier = pltpu.get_barrier_semaphore()
    for to in (Y, X, CORE):
        pl.semaphore_signal(barrier, inc=1, device_id=device[to], device_id_type=MESH)

    @pl.when(z < nz - 1)
    def _():
        pl.semaphore_signal(barrier, inc=1, device_id=device[UP], device_id_type=MESH)

    @pl.when(z > 0)
    def _():
        pl.semaphore_signal(barrier, inc=1, device_id=device[DOWN], device_id_type=MESH)

    inner = (z > 0).astype(jnp.int32) + (z < nz - 1).astype(jnp.int32)
    pl.semaphore_wait(barrier, 3 + inner)

    def ref_of(w, q, own=False):
        if isinstance(q, int) and q == PAYLOAD:
            return pay_ref if own else pays_ref.at[w]
        rows = pl.ds(pl.multiple_of(q * quarter, quarter), quarter)
        return coef_ref.at[rows] if own else full_ref.at[w, rows]

    def copy(to, zz, yy, q, own=False):
        w = index(zz, yy, core)
        return pltpu.make_async_remote_copy(
            src_ref=ref_of(w, q, own),
            dst_ref=ref_of(w, q),
            send_sem=send_sem.at[to, (zz * 2 + yy) * CHUNKS + q],
            recv_sem=recv_sem.at[w * CHUNKS + q],
            device_id=device[to],
            device_id_type=MESH,
        )

    sent = []

    def send(to, zz, yy, q, own=False, when=None):
        sent.append((to, zz, yy, q, own, when))
        copy(to, zz, yy, q, own).start()

    def arrived(w, q):
        pltpu.make_async_remote_copy(
            src_ref=ref_of(w, q),
            dst_ref=ref_of(w, q),
            send_sem=send_sem.at[CORE, 0],
            recv_sem=recv_sem.at[w * CHUNKS + q],
            device_id=device[CORE],
            device_id_type=MESH,
        ).wait_recv()

    def guarded(when, body):
        if when is None:
            body()
        else:
            pl.when(when)(body)

    first, second, third, missing = 3 * x, 1 + x, 2 - x, 3 - 3 * x
    along_z = (PAYLOAD, first, second, third)

    for q in along_z:
        for to, when in ((UP, z < nz - 1), (DOWN, z > 0)):
            guarded(when, functools.partial(send, to, z, y, q, True, when))
    for q in (PAYLOAD, first, second, third, missing):
        send(Y, z, y, q, True)
        send(CORE, z, y, q, True)
    mine = [
        pltpu.make_async_copy(coef_ref, full_ref.at[wide], local_sem.at[0]),
        pltpu.make_async_copy(pay_ref, pays_ref.at[wide], local_sem.at[1]),
    ]
    for c in mine:
        c.start()

    def sides(d):
        return ((z - d, z >= d, UP, z < nz - 1), (z + d, z + d < nz, DOWN, z > 0))

    def take_z(d):
        for q in along_z:
            for zz, valid, onward, more in sides(d):
                both = jnp.logical_and(valid, more)

                def body(zz=zz, valid=valid, onward=onward, both=both, q=q):
                    arrived(index(zz, y, core), q)
                    if d < nz - 1:
                        guarded(both, functools.partial(send, onward, zz, y, q, False, both))
                    if q is not third:
                        send(Y, zz, y, q, False, valid)
                    if q is first:
                        send(X, zz, y, q, False, valid)
                    send(CORE, zz, y, q, False, valid)

                guarded(valid, body)

    def take_y_own():
        for q in (PAYLOAD, first, second, third, missing):
            arrived(index(z, other, core), q)
            send(CORE, z, other, q)

    def take_y(d):
        for q in (PAYLOAD, first, second):
            for zz, valid, _, _ in sides(d):

                def body(zz=zz, valid=valid, q=q):
                    arrived(index(zz, other, core), q)
                    if q is not PAYLOAD:
                        send(X, zz, other, q, False, valid)
                    send(CORE, zz, other, q, False, valid)

                guarded(valid, body)

    def take_x(d):
        for yy, q in ((y, missing), (other, missing), (other, third)):
            for zz, valid, _, _ in sides(d):

                def body(zz=zz, valid=valid, q=q, yy=yy):
                    arrived(index(zz, yy, core), q)
                    send(CORE, zz, yy, q, False, valid)

                guarded(valid, body)

    for step in range(1, nz + 2):
        if step < nz:
            take_z(step)
        if step == 1:
            take_y_own()
        elif step - 1 < nz:
            take_y(step - 1)
        if 1 <= step - 2:
            take_x(step - 2)

    for zz in range(nz):
        for yy in range(2):
            for q in range(CHUNKS):
                arrived(index(zz, yy, 1 - core), q)
    for c in mine:
        c.wait()
    for to, zz, yy, q, own, when in sent:
        guarded(when, lambda: copy(to, zz, yy, q, own).wait_send())


def gather(coef, payload, wide):
    rows, columns = coef.shape
    nz = wide // 4
    return pl.pallas_call(
        functools.partial(gather_kernel, nz),
        out_shape=(
            jax.ShapeDtypeStruct((wide, rows, columns), coef.dtype),
            jax.ShapeDtypeStruct((wide,) + payload.shape, payload.dtype),
        ),
        in_specs=[pl.BlockSpec(memory_space=pl.ANY)] * 2,
        out_specs=(pl.BlockSpec(memory_space=pl.ANY),) * 2,
        scratch_shapes=[
            pltpu.SemaphoreType.DMA((5, nz * 2 * CHUNKS)),
            pltpu.SemaphoreType.DMA((wide * CHUNKS,)),
            pltpu.SemaphoreType.DMA((2,)),
        ],
        compiler_params=pltpu.CompilerParams(collective_id=0, has_side_effects=True),
        cost_estimate=pl.CostEstimate(
            flops=0, bytes_accessed=2 * wide * rows * columns * 2, transcendentals=0
        ),
    )(coef, payload)


def product_kernel(
    block, meta, pays_ref, coef_ref, full_ref, out_ref, half_ref, acc_ref, place, bra_of, start, fill
):
    slots = meta.shape[0] * 4
    places = place.shape[0]

    @pl.when(pl.program_id(0) == 0)
    def _():
        def clear(i, _):
            place[i] = -1
            bra_of[i] = 0
            return 0

        lax.fori_loop(0, places, clear, 0)
        for p in range(PAIR_COUNT):
            fill[p] = 0

        def count(s, _):
            w, r = s // 4, s % 4

            @pl.when(meta[w, 12 + r] > 0)
            def _():
                p = meta[w, r]
                fill[p] = fill[p] + 1

            return 0

        lax.fori_loop(0, slots, count, 0)
        start[0] = 0
        for p in range(PAIR_COUNT):
            start[p + 1] = start[p] + (fill[p] + 3) // 4
            fill[p] = 4 * start[p]

        def put(s, _):
            w, r = s // 4, s % 4

            @pl.when(meta[w, 12 + r] > 0)
            def _():
                p = meta[w, r]
                to = fill[p]
                place[to] = s
                bra_of[to] = meta[w, 4 + r]
                fill[p] = to + 1

            return 0

        lax.fori_loop(0, slots, put, 0)

        def make(g, _):
            parts = []
            for k in range(4):
                s = place[4 * g + k]
                at = jnp.maximum(s, 0)
                w, r = at // 4, at % 4
                two = pays_ref[w, pl.ds(pl.multiple_of((r // 2) * block, block), block), :]
                one = jnp.where(r % 2 == 0, two[:, :block], two[:, block:])
                one = jnp.where(s >= 0, one, jnp.zeros_like(one))
                ket = meta[w, 8 + r]
                rows = coef_ref[pl.ds(pl.multiple_of(ket * block, block), block), :]
                parts.append(jnp.dot(one, rows, preferred_element_type=jnp.float32))
            half_ref[g] = jnp.concatenate(parts, axis=0).T.astype(jnp.bfloat16)
            return 0

        lax.fori_loop(0, start[PAIR_COUNT], make, 0)

    tiles = full_ref.shape[0]
    width = full_ref.shape[2]

    def term(t, g):
        rows = [
            full_ref[t, pl.ds(pl.multiple_of(bra_of[4 * g + k] * block, block), block), :]
            for k in range(4)
        ]
        return jnp.dot(
            half_ref[g], jnp.concatenate(rows, axis=0), preferred_element_type=jnp.float32
        )

    for p in range(PAIR_COUNT):
        begin = start[p]
        groups = start[p + 1] - begin

        @pl.when(groups == 0)
        def _():
            out_ref[p] = jnp.zeros(out_ref.shape[1:], out_ref.dtype)

        @pl.when(groups == 1)
        def _():
            for t in range(tiles):
                out_ref[p, :, t * width : (t + 1) * width] = term(t, begin).astype(out_ref.dtype)

        @pl.when(groups == 2)
        def _():
            for t in range(tiles):
                out_ref[p, :, t * width : (t + 1) * width] = (
                    term(t, begin) + term(t, begin + 1)
                ).astype(out_ref.dtype)

        @pl.when(groups > 2)
        def _():
            for t in range(tiles):
                acc_ref[...] = term(t, begin)

                def more(g, _, t=t):
                    acc_ref[...] += term(t, g)
                    return 0

                lax.fori_loop(begin + 1, begin + groups, more, 0)
                out_ref[p, :, t * width : (t + 1) * width] = acc_ref[...].astype(out_ref.dtype)


def product(meta, pays, coef, full, block):
    wide, rows, columns = full.shape
    tiles = 2
    most = wide + PAIR_COUNT
    return pl.pallas_call(
        functools.partial(product_kernel, block),
        out_shape=jax.ShapeDtypeStruct((PAIR_COUNT, columns, wide * columns), jnp.bfloat16),
        grid_spec=pltpu.PrefetchScalarGridSpec(
            num_scalar_prefetch=1,
            grid=(wide // tiles,),
            in_specs=[
                pl.BlockSpec(pays.shape, lambda i, m: (0, 0, 0)),
                pl.BlockSpec(coef.shape, lambda i, m: (0, 0)),
                pl.BlockSpec((tiles, rows, columns), lambda i, m: (i, 0, 0)),
            ],
            out_specs=pl.BlockSpec(
                (PAIR_COUNT, columns, tiles * columns), lambda i, m: (0, 0, i)
            ),
            scratch_shapes=[
                pltpu.VMEM((most, columns, 4 * block), jnp.bfloat16),
                pltpu.VMEM((columns, columns), jnp.float32),
                pltpu.SMEM((4 * most,), jnp.int32),
                pltpu.SMEM((4 * most,), jnp.int32),
                pltpu.SMEM((PAIR_COUNT + 1,), jnp.int32),
                pltpu.SMEM((PAIR_COUNT,), jnp.int32),
            ],
        ),
        compiler_params=pltpu.CompilerParams(vmem_limit_bytes=48 * 1024 * 1024),
    )(meta, pays, coef, full)


def local(wide, xblocks, pattern, counts, coef):
    slots, block, _ = xblocks.shape
    live = (jnp.arange(slots, dtype=jnp.int32) < counts[0]).astype(jnp.int32)
    numbers = jnp.concatenate([pattern, live[None]], axis=0).astype(jnp.bfloat16)
    pairs = xblocks.reshape(slots // 2, 2, block, block).transpose(0, 2, 1, 3)
    pairs = pairs.reshape(slots // 2 * block, 2 * block)
    payload = jnp.concatenate(
        [pairs, jnp.pad(numbers, ((0, 12), (0, 2 * block - slots)))], axis=0
    )
    full, pays = gather(coef, payload, wide)
    at = slots // 2 * block
    meta = pays[:, at : at + 4, :slots].astype(jnp.int32).reshape(wide, 4 * slots)
    return product(meta, pays, coef, full, block)


def local_any(xblocks, pattern, counts, coef):
    slot_count = xblocks.shape[0]
    block_tile = xblocks.shape[1]
    column_list = coef.shape[1]
    targets_all = PAIR_COUNT * DOMAIN_BLOCKS
    active_mask = jnp.arange(slot_count, dtype=jnp.int32) < counts[0]
    destination = jnp.where(active_mask, pattern[0] * DOMAIN_BLOCKS + pattern[1], -1)
    local_rows = coef.reshape(DOMAIN_BLOCKS, block_tile, column_list)
    blocks = lax.all_gather(xblocks, "wide", axis=0, tiled=True)
    tgt = lax.all_gather(destination, "wide", axis=0, tiled=True)
    sigma = lax.all_gather(pattern[2], "wide", axis=0, tiled=True)
    picked = local_rows[sigma]
    contribution = jnp.einsum(
        "sij,sjb->sib", blocks, picked, preferred_element_type=jnp.float32
    ).astype(jnp.bfloat16)
    flattened = contribution.reshape(blocks.shape[0], block_tile * column_list)
    selector = (tgt[None, :] == jnp.arange(targets_all, dtype=jnp.int32)[:, None]).astype(
        jnp.bfloat16
    )
    half_sum = jnp.dot(selector, flattened, preferred_element_type=jnp.float32)
    half = half_sum.astype(jnp.bfloat16).reshape(
        PAIR_COUNT, DOMAIN_BLOCKS * block_tile, column_list
    )
    return jnp.einsum(
        "pnb,na->pba",
        half,
        lax.all_gather(coef, "wide", axis=1, tiled=True),
        preferred_element_type=jnp.float32,
    ).astype(jnp.bfloat16)


def solution(mesh):
    placed = (
        P(("grp", "wide"), None, None),
        P(None, ("grp", "wide")),
        P(("grp", "wide")),
        P(None, "wide"),
    )
    wide = mesh.shape["wide"]
    body = functools.partial(local, wide) if wide == 16 and mesh.shape["grp"] == 2 else local_any
    return jax.shard_map(
        body, mesh=mesh, in_specs=placed, out_specs=P("grp", "wide", None), check_vma=False
    )
```

```python
import functools

import jax
import jax.numpy as jnp
from jax import lax
from jax.experimental import pallas as pl
from jax.experimental.pallas import tpu as pltpu
from jax.sharding import PartitionSpec as P

DOMAIN_BLOCKS = 32
PAIR_COUNT = 8
MESH = pl.DeviceIdType.MESH
PAYLOAD = 4
CHUNKS = 5
UP, DOWN, Y, X, CORE = range(5)


def gather_kernel(nz, coef_ref, pay_ref, full_ref, pays_ref, send_sem, recv_sem, local_sem):
    x = lax.axis_index("grp")
    wide = lax.axis_index("wide")
    z, y, core = lax.div(wide, 4), lax.rem(lax.div(wide, 2), 2), lax.rem(wide, 2)
    other = 1 - y
    quarter = coef_ref.shape[0] // 4

    def index(zz, yy, cc):
        return (zz * 2 + yy) * 2 + cc

    device = {
        UP: {"wide": wide + 4},
        DOWN: {"wide": wide - 4},
        Y: {"wide": index(z, 1 - y, core)},
        X: {"grp": 1 - x},
        CORE: {"wide": index(z, y, 1 - core)},
    }
    barrier = pltpu.get_barrier_semaphore()
    for to in (Y, X, CORE):
        pl.semaphore_signal(barrier, inc=1, device_id=device[to], device_id_type=MESH)

    @pl.when(z < nz - 1)
    def _():
        pl.semaphore_signal(barrier, inc=1, device_id=device[UP], device_id_type=MESH)

    @pl.when(z > 0)
    def _():
        pl.semaphore_signal(barrier, inc=1, device_id=device[DOWN], device_id_type=MESH)

    inner = (z > 0).astype(jnp.int32) + (z < nz - 1).astype(jnp.int32)
    pl.semaphore_wait(barrier, 3 + inner)

    def ref_of(w, q, own=False):
        if isinstance(q, int) and q == PAYLOAD:
            return pay_ref if own else pays_ref.at[w]
        rows = pl.ds(pl.multiple_of(q * quarter, quarter), quarter)
        return coef_ref.at[rows] if own else full_ref.at[w, rows]

    def copy(to, zz, yy, q, own=False):
        w = index(zz, yy, core)
        return pltpu.make_async_remote_copy(
            src_ref=ref_of(w, q, own),
            dst_ref=ref_of(w, q),
            send_sem=send_sem.at[to, (zz * 2 + yy) * CHUNKS + q],
            recv_sem=recv_sem.at[w * CHUNKS + q],
            device_id=device[to],
            device_id_type=MESH,
        )

    sent, paced = [], []

    def send(to, zz, yy, q, own=False, when=None, group=sent):
        group.append((to, zz, yy, q, own, when))
        copy(to, zz, yy, q, own).start()

    def arrived(w, q):
        pltpu.make_async_remote_copy(
            src_ref=ref_of(w, q),
            dst_ref=ref_of(w, q),
            send_sem=send_sem.at[CORE, 0],
            recv_sem=recv_sem.at[w * CHUNKS + q],
            device_id=device[CORE],
            device_id_type=MESH,
        ).wait_recv()

    def guarded(when, body):
        if when is None:
            body()
        else:
            pl.when(when)(body)

    first, second, third, missing = 3 * x, 1 + x, 2 - x, 3 - 3 * x
    early = (PAYLOAD, first, second)

    def send_z(q):
        for to, when in ((UP, z < nz - 1), (DOWN, z > 0)):
            guarded(when, functools.partial(send, to, z, y, q, True, when))

    for q in (PAYLOAD, first, second):
        send_z(q)
        send(Y, z, y, q, True)
    for q in (PAYLOAD, first, second, third, missing):
        send(CORE, z, y, q, True)
    mine = [
        pltpu.make_async_copy(coef_ref, full_ref.at[wide], local_sem.at[0]),
        pltpu.make_async_copy(pay_ref, pays_ref.at[wide], local_sem.at[1]),
    ]
    for c in mine:
        c.start()

    def settle(group):
        for to, zz, yy, q, own, when in group:
            guarded(when, lambda: copy(to, zz, yy, q, own).wait_send())

    def sides(d):
        return ((z - d, z >= d, UP, z < nz - 1), (z + d, z + d < nz, DOWN, z > 0))

    def take_z(d, quarters):
        for q in quarters:
            for zz, valid, onward, more in sides(d):
                both = jnp.logical_and(valid, more)

                def body(zz=zz, valid=valid, onward=onward, both=both, q=q):
                    arrived(index(zz, y, core), q)
                    if d < nz - 1:
                        group = paced if d == 2 and q is not third else sent
                        guarded(both, functools.partial(send, onward, zz, y, q, False, both, group))
                    if q is not third:
                        send(Y, zz, y, q, False, valid)
                    if q is first:
                        send(X, zz, y, q, False, valid)
                    send(CORE, zz, y, q, False, valid)

                guarded(valid, body)

    def take_y_own(quarters):
        for q in quarters:
            arrived(index(z, other, core), q)
            send(CORE, z, other, q)

    def take_y(d):
        for q in (PAYLOAD, first, second):
            for zz, valid, _, _ in sides(d):

                def body(zz=zz, valid=valid, q=q):
                    arrived(index(zz, other, core), q)
                    if q is not PAYLOAD:
                        send(X, zz, other, q, False, valid)
                    send(CORE, zz, other, q, False, valid)

                guarded(valid, body)

    def take_x(d):
        for yy, q in ((y, missing), (other, missing), (other, third)):
            for zz, valid, _, _ in sides(d):

                def body(zz=zz, valid=valid, q=q, yy=yy):
                    arrived(index(zz, yy, core), q)
                    send(CORE, zz, yy, q, False, valid)

                guarded(valid, body)

    take_z(1, early)
    take_z(2, early)
    take_y_own((PAYLOAD, first, second))
    take_y(1)
    settle(paced)
    send_z(third)
    take_z(3, early)
    take_y(2)
    take_z(1, (third,))
    take_x(1)
    take_y(3)
    send(Y, z, y, third, True)
    send(Y, z, y, missing, True)
    take_z(2, (third,))
    take_x(2)
    take_z(3, (third,))
    take_y_own((third, missing))
    take_x(3)

    for zz in range(nz):
        for yy in range(2):
            for q in range(CHUNKS):
                arrived(index(zz, yy, 1 - core), q)
    for c in mine:
        c.wait()
    settle(sent)


def gather(coef, payload, wide):
    rows, columns = coef.shape
    nz = wide // 4
    return pl.pallas_call(
        functools.partial(gather_kernel, nz),
        out_shape=(
            jax.ShapeDtypeStruct((wide, rows, columns), coef.dtype),
            jax.ShapeDtypeStruct((wide,) + payload.shape, payload.dtype),
        ),
        in_specs=[pl.BlockSpec(memory_space=pl.ANY)] * 2,
        out_specs=(pl.BlockSpec(memory_space=pl.ANY),) * 2,
        scratch_shapes=[
            pltpu.SemaphoreType.DMA((5, nz * 2 * CHUNKS)),
            pltpu.SemaphoreType.DMA((wide * CHUNKS,)),
            pltpu.SemaphoreType.DMA((2,)),
        ],
        compiler_params=pltpu.CompilerParams(collective_id=0, has_side_effects=True),
        cost_estimate=pl.CostEstimate(
            flops=0, bytes_accessed=2 * wide * rows * columns * 2, transcendentals=0
        ),
    )(coef, payload)


def product_kernel(
    block, tiles, meta, pays_ref, coef_ref, full_ref, out_ref,
    held, half_ref, acc_ref, ready, place, bra_of, start, fill, in_sem, out_sem,
):
    wide, _, width = full_ref.shape

    def load(w):
        return pltpu.make_async_copy(full_ref.at[w], held.at[w], in_sem.at[w])

    for w in range(wide):
        load(w).start()

    slots = meta.shape[0] * 4
    places = place.shape[0]

    def clear(i, _):
        place[i] = -1
        bra_of[i] = 0
        return 0

    lax.fori_loop(0, places, clear, 0)
    for p in range(PAIR_COUNT):
        fill[p] = 0

    def count(s, _):
        w, r = s // 4, s % 4

        @pl.when(meta[w, 12 + r] > 0)
        def _():
            p = meta[w, r]
            fill[p] = fill[p] + 1

        return 0

    lax.fori_loop(0, slots, count, 0)
    start[0] = 0
    for p in range(PAIR_COUNT):
        start[p + 1] = start[p] + (fill[p] + 3) // 4
        fill[p] = 4 * start[p]

    def put(s, _):
        w, r = s // 4, s % 4

        @pl.when(meta[w, 12 + r] > 0)
        def _():
            p = meta[w, r]
            to = fill[p]
            place[to] = s
            bra_of[to] = meta[w, 4 + r]
            fill[p] = to + 1

        return 0

    lax.fori_loop(0, slots, put, 0)

    def make(g, _):
        parts = []
        for k in range(4):
            s = place[4 * g + k]
            at = jnp.maximum(s, 0)
            w, r = at // 4, at % 4
            two = pays_ref[w, pl.ds(pl.multiple_of((r // 2) * block, block), block), :]
            one = jnp.where(r % 2 == 0, two[:, :block], two[:, block:])
            one = jnp.where(s >= 0, one, jnp.zeros_like(one))
            ket = meta[w, 8 + r]
            rows = coef_ref[pl.ds(pl.multiple_of(ket * block, block), block), :]
            parts.append(jnp.dot(one, rows, preferred_element_type=jnp.float32))
        half_ref[g] = jnp.concatenate(parts, axis=0).T.astype(jnp.bfloat16)
        return 0

    lax.fori_loop(0, start[PAIR_COUNT], make, 0)

    span = tiles * width

    def term(i, t, g):
        rows = [
            held[i * tiles + t, pl.ds(pl.multiple_of(bra_of[4 * g + k] * block, block), block), :]
            for k in range(4)
        ]
        return jnp.dot(
            half_ref[g], jnp.concatenate(rows, axis=0), preferred_element_type=jnp.float32
        )

    def store(i, slot, p):
        columns = pl.ds(pl.multiple_of(i * span, span), span)
        return pltpu.make_async_copy(
            ready.at[slot, p], out_ref.at[p, :, columns], out_sem.at[slot, p]
        )

    def pair(i, slot, p):
        begin = start[p]
        groups = start[p + 1] - begin

        @pl.when(groups == 0)
        def _():
            ready[slot, p] = jnp.zeros(ready.shape[2:], ready.dtype)

        @pl.when(groups == 1)
        def _():
            for t in range(tiles):
                ready[slot, p, :, t * width : (t + 1) * width] = term(i, t, begin).astype(
                    ready.dtype
                )

        @pl.when(groups == 2)
        def _():
            for t in range(tiles):
                ready[slot, p, :, t * width : (t + 1) * width] = (
                    term(i, t, begin) + term(i, t, begin + 1)
                ).astype(ready.dtype)

        @pl.when(groups > 2)
        def _():
            for t in range(tiles):
                acc_ref[t] = term(i, t, begin) + term(i, t, begin + 1)

            def more(g, _):
                for t in range(tiles):
                    acc_ref[t] += term(i, t, g)
                return 0

            lax.fori_loop(begin + 2, begin + groups, more, 0)
            for t in range(tiles):
                ready[slot, p, :, t * width : (t + 1) * width] = acc_ref[t].astype(ready.dtype)

    count_of = wide // tiles

    def strip(i, _):
        slot = lax.rem(i, 2)
        for t in range(tiles):
            load(i * tiles + t).wait()

        def one(p, _):
            @pl.when(i >= 2)
            def _():
                store(i - 2, slot, p).wait()

            pair(i, slot, p)
            store(i, slot, p).start()
            return 0

        lax.fori_loop(0, PAIR_COUNT, one, 0)
        return 0

    lax.fori_loop(0, count_of, strip, 0)
    for i in (count_of - 2, count_of - 1):
        for p in range(PAIR_COUNT):
            store(i, i % 2, p).wait()


def product(meta, pays, coef, full, block):
    wide, rows, columns = full.shape
    tiles = 4
    most = wide + PAIR_COUNT
    whole = pl.BlockSpec(memory_space=pltpu.VMEM)
    return pl.pallas_call(
        functools.partial(product_kernel, block, tiles),
        out_shape=jax.ShapeDtypeStruct((PAIR_COUNT, columns, wide * columns), jnp.bfloat16),
        in_specs=[
            pl.BlockSpec(memory_space=pltpu.SMEM),
            whole,
            whole,
            pl.BlockSpec(memory_space=pl.ANY),
        ],
        out_specs=pl.BlockSpec(memory_space=pl.ANY),
        scratch_shapes=[
            pltpu.VMEM(full.shape, full.dtype),
            pltpu.VMEM((most, columns, 4 * block), jnp.bfloat16),
            pltpu.VMEM((tiles, columns, columns), jnp.float32),
            pltpu.VMEM((2, PAIR_COUNT, columns, tiles * columns), jnp.bfloat16),
            pltpu.SMEM((4 * most,), jnp.int32),
            pltpu.SMEM((4 * most,), jnp.int32),
            pltpu.SMEM((PAIR_COUNT + 1,), jnp.int32),
            pltpu.SMEM((PAIR_COUNT,), jnp.int32),
            pltpu.SemaphoreType.DMA((wide,)),
            pltpu.SemaphoreType.DMA((2, PAIR_COUNT)),
        ],
        compiler_params=pltpu.CompilerParams(vmem_limit_bytes=48 * 1024 * 1024),
    )(meta, pays, coef, full)


def local(wide, xblocks, pattern, counts, coef):
    slots, block, _ = xblocks.shape
    live = (jnp.arange(slots, dtype=jnp.int32) < counts[0]).astype(jnp.int32)
    numbers = jnp.concatenate([pattern, live[None]], axis=0).astype(jnp.bfloat16)
    pairs = xblocks.reshape(slots // 2, 2, block, block).transpose(0, 2, 1, 3)
    pairs = pairs.reshape(slots // 2 * block, 2 * block)
    payload = jnp.concatenate(
        [pairs, jnp.pad(numbers, ((0, 12), (0, 2 * block - slots)))], axis=0
    )
    full, pays = gather(coef, payload, wide)
    at = slots // 2 * block
    meta = pays[:, at : at + 4, :slots].astype(jnp.int32).reshape(wide, 4 * slots)
    return product(meta, pays, coef, full, block)


def local_any(xblocks, pattern, counts, coef):
    slot_count = xblocks.shape[0]
    block_tile = xblocks.shape[1]
    column_list = coef.shape[1]
    targets_all = PAIR_COUNT * DOMAIN_BLOCKS
    active_mask = jnp.arange(slot_count, dtype=jnp.int32) < counts[0]
    destination = jnp.where(active_mask, pattern[0] * DOMAIN_BLOCKS + pattern[1], -1)
    local_rows = coef.reshape(DOMAIN_BLOCKS, block_tile, column_list)
    blocks = lax.all_gather(xblocks, "wide", axis=0, tiled=True)
    tgt = lax.all_gather(destination, "wide", axis=0, tiled=True)
    sigma = lax.all_gather(pattern[2], "wide", axis=0, tiled=True)
    picked = local_rows[sigma]
    contribution = jnp.einsum(
        "sij,sjb->sib", blocks, picked, preferred_element_type=jnp.float32
    ).astype(jnp.bfloat16)
    flattened = contribution.reshape(blocks.shape[0], block_tile * column_list)
    selector = (tgt[None, :] == jnp.arange(targets_all, dtype=jnp.int32)[:, None]).astype(
        jnp.bfloat16
    )
    half_sum = jnp.dot(selector, flattened, preferred_element_type=jnp.float32)
    half = half_sum.astype(jnp.bfloat16).reshape(
        PAIR_COUNT, DOMAIN_BLOCKS * block_tile, column_list
    )
    return jnp.einsum(
        "pnb,na->pba",
        half,
        lax.all_gather(coef, "wide", axis=1, tiled=True),
        preferred_element_type=jnp.float32,
    ).astype(jnp.bfloat16)


def solution(mesh):
    placed = (
        P(("grp", "wide"), None, None),
        P(None, ("grp", "wide")),
        P(("grp", "wide")),
        P(None, "wide"),
    )
    wide = mesh.shape["wide"]
    body = functools.partial(local, wide) if wide == 16 and mesh.shape["grp"] == 2 else local_any
    return jax.shard_map(
        body, mesh=mesh, in_specs=placed, out_specs=P("grp", "wide", None), check_vma=False
    )
```

```python
import functools

import jax
import jax.numpy as jnp
from jax import lax
from jax.experimental import pallas as pl
from jax.experimental.pallas import tpu as pltpu
from jax.sharding import PartitionSpec as P

DOMAIN_BLOCKS = 32
PAIR_COUNT = 8
MESH = pl.DeviceIdType.MESH
PAYLOAD = 4
CHUNKS = 5
UP, DOWN, Y, X, CORE = range(5)


def gather_kernel(nz, coef_ref, pay_ref, full_ref, pays_ref, send_sem, recv_sem, local_sem):
    x = lax.axis_index("grp")
    wide = lax.axis_index("wide")
    z, y, core = lax.div(wide, 4), lax.rem(lax.div(wide, 2), 2), lax.rem(wide, 2)
    other = 1 - y
    quarter = coef_ref.shape[0] // 4

    def index(zz, yy, cc):
        return (zz * 2 + yy) * 2 + cc

    device = {
        UP: {"wide": wide + 4},
        DOWN: {"wide": wide - 4},
        Y: {"wide": index(z, 1 - y, core)},
        X: {"grp": 1 - x},
        CORE: {"wide": index(z, y, 1 - core)},
    }
    barrier = pltpu.get_barrier_semaphore()
    for to in (Y, X, CORE):
        pl.semaphore_signal(barrier, inc=1, device_id=device[to], device_id_type=MESH)

    @pl.when(z < nz - 1)
    def _():
        pl.semaphore_signal(barrier, inc=1, device_id=device[UP], device_id_type=MESH)

    @pl.when(z > 0)
    def _():
        pl.semaphore_signal(barrier, inc=1, device_id=device[DOWN], device_id_type=MESH)

    inner = (z > 0).astype(jnp.int32) + (z < nz - 1).astype(jnp.int32)
    pl.semaphore_wait(barrier, 3 + inner)

    def ref_of(w, q, own=False):
        if isinstance(q, int) and q == PAYLOAD:
            return pay_ref if own else pays_ref.at[w]
        rows = pl.ds(pl.multiple_of(q * quarter, quarter), quarter)
        return coef_ref.at[rows] if own else full_ref.at[w, rows]

    def copy(to, zz, yy, q, own=False):
        w = index(zz, yy, core)
        return pltpu.make_async_remote_copy(
            src_ref=ref_of(w, q, own),
            dst_ref=ref_of(w, q),
            send_sem=send_sem.at[to, (zz * 2 + yy) * CHUNKS + q],
            recv_sem=recv_sem.at[w * CHUNKS + q],
            device_id=device[to],
            device_id_type=MESH,
        )

    sent, paced = [], []

    def send(to, zz, yy, q, own=False, when=None, group=sent):
        group.append((to, zz, yy, q, own, when))
        copy(to, zz, yy, q, own).start()

    def arrived(w, q):
        pltpu.make_async_remote_copy(
            src_ref=ref_of(w, q),
            dst_ref=ref_of(w, q),
            send_sem=send_sem.at[CORE, 0],
            recv_sem=recv_sem.at[w * CHUNKS + q],
            device_id=device[CORE],
            device_id_type=MESH,
        ).wait_recv()

    def guarded(when, body):
        if when is None:
            body()
        else:
            pl.when(when)(body)

    first, second, third, missing = 3 * x, 1 + x, 2 - x, 3 - 3 * x
    early = (PAYLOAD, first, second)

    def send_z(q):
        for to, when in ((UP, z < nz - 1), (DOWN, z > 0)):
            guarded(when, functools.partial(send, to, z, y, q, True, when))

    for q in (PAYLOAD, first, second):
        send_z(q)
        send(Y, z, y, q, True)
    for q in (PAYLOAD, first, second, third, missing):
        send(CORE, z, y, q, True)
    mine = [
        pltpu.make_async_copy(coef_ref, full_ref.at[wide], local_sem.at[0]),
        pltpu.make_async_copy(pay_ref, pays_ref.at[wide], local_sem.at[1]),
    ]
    for c in mine:
        c.start()

    def settle(group):
        for to, zz, yy, q, own, when in group:
            guarded(when, lambda: copy(to, zz, yy, q, own).wait_send())

    def sides(d):
        return ((z - d, z >= d, UP, z < nz - 1), (z + d, z + d < nz, DOWN, z > 0))

    def take_z(d, quarters):
        for q in quarters:
            for zz, valid, onward, more in sides(d):
                both = jnp.logical_and(valid, more)

                def body(zz=zz, valid=valid, onward=onward, both=both, q=q):
                    arrived(index(zz, y, core), q)
                    if d < nz - 1:
                        group = paced if d == 2 and q is not third else sent
                        guarded(both, functools.partial(send, onward, zz, y, q, False, both, group))
                    if q is not third:
                        send(Y, zz, y, q, False, valid)
                    if q is first:
                        send(X, zz, y, q, False, valid)
                    send(CORE, zz, y, q, False, valid)

                guarded(valid, body)

    def take_y_own(quarters):
        for q in quarters:
            arrived(index(z, other, core), q)
            send(CORE, z, other, q)

    def take_y(d):
        for q in (PAYLOAD, first, second):
            for zz, valid, _, _ in sides(d):

                def body(zz=zz, valid=valid, q=q):
                    arrived(index(zz, other, core), q)
                    if q is not PAYLOAD:
                        send(X, zz, other, q, False, valid)
                    send(CORE, zz, other, q, False, valid)

                guarded(valid, body)

    def take_x(d):
        for yy, q in ((y, missing), (other, missing), (other, third)):
            for zz, valid, _, _ in sides(d):

                def body(zz=zz, valid=valid, q=q, yy=yy):
                    arrived(index(zz, yy, core), q)
                    send(CORE, zz, yy, q, False, valid)

                guarded(valid, body)

    take_z(1, early)
    take_z(2, early)
    take_y_own((PAYLOAD, first, second))
    take_y(1)
    settle(paced)
    send_z(third)
    take_z(3, early)
    take_y(2)
    take_z(1, (third,))
    take_x(1)
    take_y(3)
    send(Y, z, y, third, True)
    send(Y, z, y, missing, True)
    take_z(2, (third,))
    take_x(2)
    take_z(3, (third,))
    take_y_own((third, missing))
    take_x(3)

    for zz in range(nz):
        for yy in range(2):
            for q in range(CHUNKS):
                arrived(index(zz, yy, 1 - core), q)
    for c in mine:
        c.wait()
    settle(sent)


def gather(coef, payload, wide):
    rows, columns = coef.shape
    nz = wide // 4
    return pl.pallas_call(
        functools.partial(gather_kernel, nz),
        out_shape=(
            jax.ShapeDtypeStruct((wide, rows, columns), coef.dtype),
            jax.ShapeDtypeStruct((wide,) + payload.shape, payload.dtype),
        ),
        in_specs=[pl.BlockSpec(memory_space=pl.ANY)] * 2,
        out_specs=(pl.BlockSpec(memory_space=pl.ANY),) * 2,
        scratch_shapes=[
            pltpu.SemaphoreType.DMA((5, nz * 2 * CHUNKS)),
            pltpu.SemaphoreType.DMA((wide * CHUNKS,)),
            pltpu.SemaphoreType.DMA((2,)),
        ],
        compiler_params=pltpu.CompilerParams(collective_id=0, has_side_effects=True),
        cost_estimate=pl.CostEstimate(
            flops=0, bytes_accessed=2 * wide * rows * columns * 2, transcendentals=0
        ),
    )(coef, payload)


def product_kernel(
    block, tiles, meta, pays_ref, coef_ref, full_ref, out_ref,
    held, half_ref, acc_ref, ready, place, bra_of, start, fill, in_sem, out_sem,
):
    wide, _, width = full_ref.shape

    def load(w):
        return pltpu.make_async_copy(full_ref.at[w], held.at[w], in_sem.at[w])

    for w in range(wide):
        load(w).start()

    slots = meta.shape[0] * 4
    places = place.shape[0]

    def clear(i, _):
        place[i] = -1
        bra_of[i] = 0
        return 0

    lax.fori_loop(0, places, clear, 0)
    for p in range(PAIR_COUNT):
        fill[p] = 0

    def count(s, _):
        w, r = s // 4, s % 4

        @pl.when(meta[w, 12 + r] > 0)
        def _():
            p = meta[w, r]
            fill[p] = fill[p] + 1

        return 0

    lax.fori_loop(0, slots, count, 0)
    start[0] = 0
    for p in range(PAIR_COUNT):
        start[p + 1] = start[p] + (fill[p] + 3) // 4
        fill[p] = 4 * start[p]

    def put(s, _):
        w, r = s // 4, s % 4

        @pl.when(meta[w, 12 + r] > 0)
        def _():
            p = meta[w, r]
            to = fill[p]
            place[to] = s
            bra_of[to] = meta[w, 4 + r]
            fill[p] = to + 1

        return 0

    lax.fori_loop(0, slots, put, 0)

    def make(g, _):
        parts = []
        for k in range(4):
            s = place[4 * g + k]
            at = jnp.maximum(s, 0)
            w, r = at // 4, at % 4
            two = pays_ref[w, pl.ds(pl.multiple_of((r // 2) * block, block), block), :]
            one = jnp.where(r % 2 == 0, two[:, :block], two[:, block:])
            one = jnp.where(s >= 0, one, jnp.zeros_like(one))
            ket = meta[w, 8 + r]
            rows = coef_ref[pl.ds(pl.multiple_of(ket * block, block), block), :]
            parts.append(jnp.dot(one, rows, preferred_element_type=jnp.float32))
        half_ref[g] = jnp.concatenate(parts, axis=0).T.astype(jnp.bfloat16)
        return 0

    lax.fori_loop(0, start[PAIR_COUNT], make, 0)

    span = tiles * width

    def term(i, t, g):
        rows = [
            held[i * tiles + t, pl.ds(pl.multiple_of(bra_of[4 * g + k] * block, block), block), :]
            for k in range(4)
        ]
        return jnp.dot(
            half_ref[g], jnp.concatenate(rows, axis=0), preferred_element_type=jnp.float32
        )

    def store(i, slot, p):
        columns = pl.ds(pl.multiple_of(i * span, span), span)
        return pltpu.make_async_copy(
            ready.at[slot, p], out_ref.at[p, :, columns], out_sem.at[slot, p]
        )

    def pair(i, slot, p):
        begin = start[p]
        groups = start[p + 1] - begin

        @pl.when(groups == 0)
        def _():
            ready[slot, p] = jnp.zeros(ready.shape[2:], ready.dtype)

        @pl.when(groups == 1)
        def _():
            for t in range(tiles):
                ready[slot, p, :, t * width : (t + 1) * width] = term(i, t, begin).astype(
                    ready.dtype
                )

        @pl.when(groups == 2)
        def _():
            for t in range(tiles):
                ready[slot, p, :, t * width : (t + 1) * width] = (
                    term(i, t, begin) + term(i, t, begin + 1)
                ).astype(ready.dtype)

        @pl.when(groups > 2)
        def _():
            for t in range(tiles):
                acc_ref[t] = term(i, t, begin) + term(i, t, begin + 1)

            def more(g, _):
                for t in range(tiles):
                    acc_ref[t] += term(i, t, g)
                return 0

            lax.fori_loop(begin + 2, begin + groups, more, 0)
            for t in range(tiles):
                ready[slot, p, :, t * width : (t + 1) * width] = acc_ref[t].astype(ready.dtype)

    count_of = wide // tiles

    def strip(i, _):
        slot = lax.rem(i, 2)
        for t in range(tiles):
            load(i * tiles + t).wait()

        def one(p, _):
            @pl.when(i >= 2)
            def _():
                store(i - 2, slot, p).wait()

            pair(i, slot, p)
            store(i, slot, p).start()
            return 0

        lax.fori_loop(0, PAIR_COUNT, one, 0)
        return 0

    lax.fori_loop(0, count_of, strip, 0)
    for i in (count_of - 2, count_of - 1):
        for p in range(PAIR_COUNT):
            store(i, i % 2, p).wait()


def product(meta, pays, coef, full, block):
    wide, rows, columns = full.shape
    tiles = 8
    most = wide + PAIR_COUNT
    whole = pl.BlockSpec(memory_space=pltpu.VMEM)
    return pl.pallas_call(
        functools.partial(product_kernel, block, tiles),
        out_shape=jax.ShapeDtypeStruct((PAIR_COUNT, columns, wide * columns), jnp.bfloat16),
        in_specs=[
            pl.BlockSpec(memory_space=pltpu.SMEM),
            whole,
            whole,
            pl.BlockSpec(memory_space=pl.ANY),
        ],
        out_specs=pl.BlockSpec(memory_space=pl.ANY),
        scratch_shapes=[
            pltpu.VMEM(full.shape, full.dtype),
            pltpu.VMEM((most, columns, 4 * block), jnp.bfloat16),
            pltpu.VMEM((tiles, columns, columns), jnp.float32),
            pltpu.VMEM((2, PAIR_COUNT, columns, tiles * columns), jnp.bfloat16),
            pltpu.SMEM((4 * most,), jnp.int32),
            pltpu.SMEM((4 * most,), jnp.int32),
            pltpu.SMEM((PAIR_COUNT + 1,), jnp.int32),
            pltpu.SMEM((PAIR_COUNT,), jnp.int32),
            pltpu.SemaphoreType.DMA((wide,)),
            pltpu.SemaphoreType.DMA((2, PAIR_COUNT)),
        ],
        compiler_params=pltpu.CompilerParams(vmem_limit_bytes=48 * 1024 * 1024),
    )(meta, pays, coef, full)


def local(wide, xblocks, pattern, counts, coef):
    slots, block, _ = xblocks.shape
    live = (jnp.arange(slots, dtype=jnp.int32) < counts[0]).astype(jnp.int32)
    numbers = jnp.concatenate([pattern, live[None]], axis=0).astype(jnp.bfloat16)
    pairs = xblocks.reshape(slots // 2, 2, block, block).transpose(0, 2, 1, 3)
    pairs = pairs.reshape(slots // 2 * block, 2 * block)
    payload = jnp.concatenate(
        [pairs, jnp.pad(numbers, ((0, 12), (0, 2 * block - slots)))], axis=0
    )
    full, pays = gather(coef, payload, wide)
    at = slots // 2 * block
    meta = pays[:, at : at + 4, :slots].astype(jnp.int32).reshape(wide, 4 * slots)
    return product(meta, pays, coef, full, block)


def local_any(xblocks, pattern, counts, coef):
    slot_count = xblocks.shape[0]
    block_tile = xblocks.shape[1]
    column_list = coef.shape[1]
    targets_all = PAIR_COUNT * DOMAIN_BLOCKS
    active_mask = jnp.arange(slot_count, dtype=jnp.int32) < counts[0]
    destination = jnp.where(active_mask, pattern[0] * DOMAIN_BLOCKS + pattern[1], -1)
    local_rows = coef.reshape(DOMAIN_BLOCKS, block_tile, column_list)
    blocks = lax.all_gather(xblocks, "wide", axis=0, tiled=True)
    tgt = lax.all_gather(destination, "wide", axis=0, tiled=True)
    sigma = lax.all_gather(pattern[2], "wide", axis=0, tiled=True)
    picked = local_rows[sigma]
    contribution = jnp.einsum(
        "sij,sjb->sib", blocks, picked, preferred_element_type=jnp.float32
    ).astype(jnp.bfloat16)
    flattened = contribution.reshape(blocks.shape[0], block_tile * column_list)
    selector = (tgt[None, :] == jnp.arange(targets_all, dtype=jnp.int32)[:, None]).astype(
        jnp.bfloat16
    )
    half_sum = jnp.dot(selector, flattened, preferred_element_type=jnp.float32)
    half = half_sum.astype(jnp.bfloat16).reshape(
        PAIR_COUNT, DOMAIN_BLOCKS * block_tile, column_list
    )
    return jnp.einsum(
        "pnb,na->pba",
        half,
        lax.all_gather(coef, "wide", axis=1, tiled=True),
        preferred_element_type=jnp.float32,
    ).astype(jnp.bfloat16)


def solution(mesh):
    placed = (
        P(("grp", "wide"), None, None),
        P(None, ("grp", "wide")),
        P(("grp", "wide")),
        P(None, "wide"),
    )
    wide = mesh.shape["wide"]
    body = functools.partial(local, wide) if wide == 16 and mesh.shape["grp"] == 2 else local_any
    return jax.shard_map(
        body, mesh=mesh, in_specs=placed, out_specs=P("grp", "wide", None), check_vma=False
    )
```
